32 devices in a mesh: groups: 2 (over y), dom: 8 (over z, x), sub: 2 (over core).
Axes of the slice: x: 2, y: 2, z: 4, core: 2. Of those that a mesh axis runs over, the one named last changes fastest.
Arguments:
- features: bfloat16 [524288, 128], P(('groups', 'dom', 'sub')), parts along dimension 0, may hold values from -6 to 6
- fine_nbrs: int32 [6, 524288], P(None, ('groups', 'dom', 'sub')), parts along dimension 1, may hold values from 0 to 17919
- send_rows: int32 [16384], P(('groups', 'dom', 'sub')), parts along dimension 0, may hold values from 0 to 16383
- cluster: int32 [524288], P(('groups', 'dom', 'sub')), parts along dimension 0, may hold values from 0 to 32767, as said below
- coarse_send: int32 [8192], P(('groups', 'dom', 'sub')), parts along dimension 0, may hold values from 0 to 2047
- coarse_nbrs: int32 [6, 65536], P(None, ('groups', 'dom', 'sub')), parts along dimension 1, may hold values from 0 to 2815
- edge_weights: bfloat16 [2, 3, 128, 128], replicated, may hold values from -0.5 to 0.5
- node_weights: bfloat16 [2, 3, 128, 128], replicated, may hold values from -0.5 to 0.5
- biases: float32 [2, 2, 128], replicated, may hold values from -3 to 3
Outputs:
- nodes: bfloat16 [524288, 128], P(('groups', 'dom', 'sub')), parts along dimension 0
- coarse_update: bfloat16 [65536, 128], P(('groups', 'dom', 'sub')), parts along dimension 0
The draws below stay inside these ranges and needn't reach their ends.
There are 2 independent parts, one for each index of `groups`. The reference program is written for one: setup_inputs(seed, part) draws one part's arguments, and reference() takes and returns one part's arrays. A program takes and returns all parts, laid end to end along the dimension named above; an argument that names none is the same for every part. Nothing has to cross between parts.
Inputs may be any that keep to these rules, and one draw needn't show every extreme that they name: `cluster`: every coarse node has exactly 8 fine nodes. Coarse node c belongs to partition c // 2048. Of the fine nodes of partition p, exactly 14848 have their coarse node in partition p, and exactly 512 in partition p + k modulo 16, for each k = 1 .. 3.
All inputs are finite; a program needn't handle non-finite values.
Results may differ from the reference program's by a relative error of at most 0.019.
Values may be sent and summed in bfloat16 or wider, within the bound.
A program may use at most 128 MiB of HBM per device.

```python
import jax
import jax.numpy as jnp
from jax import lax

WIDTH = 128
NODE_DEV = 16384
HALO = 512
DEGREE = 6
COARSE_DEGREE = 6
RATIO = 8
REACH = 4
PARTITIONS = 16
NODES = 262144
COARSE_DEV = 2048
COARSE = 32768
HALO_ALL = 8192
COARSE_HALO = 256
COARSE_HALO_ALL = 4096
SPILL = 512


def draw_cluster(key, part):
    halves = jax.random.split(jax.random.fold_in(key, 11), 2)
    place_keys = jax.random.split(halves[0], PARTITIONS)
    order_keys = jax.random.split(halves[1], PARTITIONS)
    placed = jax.vmap(lambda single: jax.random.permutation(single, NODE_DEV))(place_keys).astype(jnp.int32)
    orders = jax.vmap(lambda single: jax.random.permutation(single, NODE_DEV))(order_keys).astype(jnp.int32)
    local_count = NODE_DEV - (REACH - 1) * SPILL
    reach_index = jnp.where(placed < local_count, 0, 1 + (placed - local_count) // SPILL).astype(jnp.int32)
    partition = jnp.arange(PARTITIONS, dtype=jnp.int32)[:, None]
    owner_part = (partition + reach_index) % PARTITIONS
    local_slot = orders[owner_part, placed] // RATIO
    return (owner_part * COARSE_DEV + local_slot).reshape(-1).astype(jnp.int32)


def plant(entries, key, low, high):
    spot = [jax.random.randint(jax.random.fold_in(key, axis), (), 0, length) for axis, length in enumerate(entries.shape)]
    widest = entries.shape.index(max(entries.shape))
    beside = spot[:widest] + [(spot[widest] + 1) % entries.shape[widest]] + spot[widest + 1:]
    return entries.at[tuple(spot)].set(low).at[tuple(beside)].set(high)


def level_of(rng, extent, pieces, least, largest):
    gain = 1.0
    for dim, blocks in pieces:
        draws = jax.random.uniform(jax.random.fold_in(jax.random.fold_in(rng, 6), dim), (blocks,), jnp.float32, least / len(pieces), largest / len(pieces))
        gain = gain * jnp.repeat(jnp.exp(draws), extent[dim] // blocks).reshape((-1,) + (1,) * (len(extent) - 1 - dim))
    return gain


def normal_values(own_key, shape, scale, reach, cuts=(), kind=jnp.bfloat16):
    drawn = scale * jax.random.normal(own_key, shape, jnp.float32)
    if cuts:
        drawn = drawn * level_of(own_key, shape, cuts, -0.22, 0.18)
    return jnp.clip(drawn, -reach, reach).astype(kind)


def setup_inputs(seed: int = 0, part: int = 0) -> dict:
    arg_keys = jax.random.split(jax.random.key(seed), 10)
    own_keys = jax.random.split(jax.random.fold_in(arg_keys[9], part), 10)
    features = normal_values(own_keys[0], (NODES, WIDTH), 1.0, 6.0, ((0, 16),))
    fine_nbrs = plant(jax.random.randint(own_keys[1], (DEGREE, NODES), 0, NODE_DEV + 3 * HALO), jax.random.fold_in(own_keys[1], 1), 0, (NODE_DEV + 3 * HALO) - 1).astype(jnp.int32)
    send_rows = plant(jax.random.randint(own_keys[2], (HALO_ALL,), 0, NODE_DEV), jax.random.fold_in(own_keys[2], 1), 0, NODE_DEV - 1).astype(jnp.int32)
    cluster = draw_cluster(jax.random.fold_in(jax.random.fold_in(arg_keys[9], part), 71), part)
    coarse_send = plant(jax.random.randint(own_keys[4], (COARSE_HALO_ALL,), 0, COARSE_DEV), jax.random.fold_in(own_keys[4], 1), 0, COARSE_DEV - 1).astype(jnp.int32)
    coarse_nbrs = plant(jax.random.randint(own_keys[5], (COARSE_DEGREE, COARSE), 0, COARSE_DEV + 3 * COARSE_HALO), jax.random.fold_in(own_keys[5], 1), 0, (COARSE_DEV + 3 * COARSE_HALO) - 1).astype(jnp.int32)
    edge_weights = normal_values(arg_keys[6], (2, 3, WIDTH, WIDTH), WIDTH ** -0.5, 0.5)
    node_weights = normal_values(arg_keys[7], (2, 3, WIDTH, WIDTH), WIDTH ** -0.5, 0.5)
    biases = normal_values(arg_keys[8], (2, 2, WIDTH), 0.5, 3.0, (), jnp.float32)
    return dict(features=features, fine_nbrs=fine_nbrs, send_rows=send_rows, cluster=cluster, coarse_send=coarse_send, coarse_nbrs=coarse_nbrs, edge_weights=edge_weights, node_weights=node_weights, biases=biases)


def message_layer(states, table, neighbor_idx, edge_proj, node_proj, bias_pair):
    count_rows = states.shape[0]
    block_rows = min(2048, count_rows)
    num_blocks = count_rows // block_rows
    far_term = jnp.dot(table, edge_proj[1], preferred_element_type=jnp.float32)
    second = edge_proj[2].astype(jnp.float32)

    def one_block(block_index):
        row_block = lax.dynamic_slice_in_dim(states, block_index * block_rows, block_rows, 0)
        nbr_block = lax.dynamic_slice_in_dim(neighbor_idx, block_index * block_rows, block_rows, 1)
        own_term = jnp.dot(row_block, edge_proj[0], preferred_element_type=jnp.float32)
        pre_act = own_term[None] + far_term[nbr_block] + bias_pair[0]
        hidden = jax.nn.silu(pre_act).astype(jnp.bfloat16)
        messages = jax.nn.silu(jnp.einsum("kbh,hg->kbg", hidden.astype(jnp.float32), second))
        gathered_msgs = jnp.sum(messages, axis=0).astype(jnp.bfloat16)
        inner = jax.nn.silu(jnp.dot(row_block, node_proj[0], preferred_element_type=jnp.float32)
                            + jnp.dot(gathered_msgs, node_proj[1], preferred_element_type=jnp.float32)
                            + bias_pair[1]).astype(jnp.bfloat16)
        return jnp.dot(inner, node_proj[2], preferred_element_type=jnp.float32)

    result = lax.map(one_block, jnp.arange(num_blocks, dtype=jnp.int32))
    return result.reshape(count_rows, -1)


def reference(features, fine_nbrs, send_rows, cluster, coarse_send, coarse_nbrs, edge_weights, node_weights, biases):
    states = features.reshape(PARTITIONS, NODE_DEV, WIDTH)
    sends = send_rows.reshape(PARTITIONS, HALO)
    outgoing = jax.vmap(lambda shard_rows, send_idx: shard_rows[send_idx])(states, sends)
    halo_rows = jnp.concatenate([jnp.roll(outgoing, 1, axis=0), outgoing, jnp.roll(outgoing, -1, axis=0)], axis=1)
    tables = jnp.concatenate([states, halo_rows], axis=1)
    nbr_parts = fine_nbrs.reshape(DEGREE, PARTITIONS, NODE_DEV).transpose(1, 0, 2)

    def fine_part(operand):
        state_part, table_part, nbr_part = operand
        update = message_layer(state_part, table_part, nbr_part, edge_weights[0], node_weights[0], biases[0])
        return (state_part.astype(jnp.float32) + update).astype(jnp.bfloat16)

    fine_out = lax.map(fine_part, (states, tables, nbr_parts))
    flat = fine_out.reshape(NODES, WIDTH)
    cluster_sum = jax.ops.segment_sum(flat.astype(jnp.float32), cluster, num_segments=COARSE)
    coarse_in = (cluster_sum * (1.0 / RATIO)).astype(jnp.bfloat16).reshape(PARTITIONS, COARSE_DEV, WIDTH)
    coarse_sends = coarse_send.reshape(PARTITIONS, COARSE_HALO)
    coarse_out = jax.vmap(lambda shard_rows, send_idx: shard_rows[send_idx])(coarse_in, coarse_sends)
    coarse_halo = jnp.concatenate([jnp.roll(coarse_out, 1, axis=0), coarse_out, jnp.roll(coarse_out, -1, axis=0)], axis=1)
    coarse_tables = jnp.concatenate([coarse_in, coarse_halo], axis=1)
    coarse_parts = coarse_nbrs.reshape(COARSE_DEGREE, PARTITIONS, COARSE_DEV).transpose(1, 0, 2)

    def coarse_part(operand):
        state_part, table_part, nbr_part = operand
        update = message_layer(state_part, table_part, nbr_part, edge_weights[1], node_weights[1], biases[1])
        return update.astype(jnp.bfloat16)

    coarse_update = lax.map(coarse_part, (coarse_in, coarse_tables, coarse_parts)).reshape(COARSE, WIDTH)
    nodes = (flat.astype(jnp.float32) + coarse_update[cluster].astype(jnp.float32)).astype(jnp.bfloat16)
    return nodes, coarse_update
```

```python
import functools

import jax
import jax.numpy as jnp
from jax import lax
from jax.experimental import pallas as pl
from jax.experimental.pallas import tpu as pltpu
from jax.sharding import PartitionSpec as P

RATIO = 8
REACH = 4
AXES = ("dom", "sub")
VMEM_LIMIT = 48 * 1024 * 1024
CHUNK = 64


def half_silu(half):
    return half + half * jnp.tanh(half)


def layer_kernel(
    degree, rows, keep, idx_ref, z_ref, far_ref, own_ref, mid_ref, mix_ref, last_ref, bias_ref, out_ref, even, odd
):
    count = rows // CHUNK

    def gather(chunk, target):
        base = chunk * CHUNK
        for k in range(degree):
            for j in range(CHUNK):
                r = k * CHUNK + j
                target[r : r + 1, :] = far_ref[idx_ref[base + (k * rows + j)]]

    def compute(chunk, source):
        start = pl.multiple_of(chunk * CHUNK, CHUNK)
        z = z_ref[pl.ds(start, CHUNK), :]
        both = jnp.dot(z, own_ref[...], preferred_element_type=jnp.float32)
        width = z.shape[1]
        own = 0.5 * (both[:, :width] + bias_ref[0:1, :])
        node = both[:, width:] + bias_ref[1:2, :]
        hidden = [
            half_silu(source[k * CHUNK : (k + 1) * CHUNK, :] + own).astype(jnp.bfloat16)
            for k in range(degree)
        ]
        msg = half_silu(
            0.5
            * jnp.dot(
                jnp.concatenate(hidden, axis=0), mid_ref[...], preferred_element_type=jnp.float32
            )
        )
        agg = msg[:CHUNK]
        for k in range(1, degree):
            agg = agg + msg[k * CHUNK : (k + 1) * CHUNK]
        pre = node + jnp.dot(
            agg.astype(jnp.bfloat16), mix_ref[...], preferred_element_type=jnp.float32
        )
        inner = half_silu(0.5 * pre).astype(jnp.bfloat16)
        update = jnp.dot(inner, last_ref[...], preferred_element_type=jnp.float32)
        if keep:
            update = (z.astype(jnp.float32) + update).astype(jnp.bfloat16)
        out_ref[pl.ds(start, CHUNK), :] = update.astype(out_ref.dtype)

    gather(0, even)

    def pair(p, carry):
        first = p * 2
        gather(first + 1, odd)
        compute(first, even)
        gather(jnp.minimum(first + 2, count - 1), even)
        compute(first + 1, odd)
        return carry

    lax.fori_loop(0, count // 2, pair, 0)


def message_layer(states, table, neighbor_idx, edge_proj, node_proj, bias_pair, keep):
    count_rows, width = states.shape
    degree = neighbor_idx.shape[0]
    rows = min(2048, count_rows)
    blocks = count_rows // rows
    far = 0.5 * jnp.dot(table, edge_proj[1], preferred_element_type=jnp.float32)
    far = far.reshape(table.shape[0], 1, width)
    order = neighbor_idx.reshape(degree, blocks, rows).transpose(1, 0, 2).reshape(-1)
    own = jnp.concatenate([edge_proj[0], node_proj[0]], axis=1)
    whole = pl.BlockSpec(memory_space=pltpu.VMEM)
    edges = count_rows * degree
    return pl.pallas_call(
        functools.partial(layer_kernel, degree, rows, keep),
        grid=(blocks,),
        in_specs=[
            pl.BlockSpec((degree * rows,), lambda i: (i,), memory_space=pltpu.SMEM),
            pl.BlockSpec((rows, width), lambda i: (i, 0)),
            whole,
            whole,
            whole,
            whole,
            whole,
            whole,
        ],
        out_specs=pl.BlockSpec((rows, width), lambda i: (i, 0)),
        out_shape=jax.ShapeDtypeStruct(
            (count_rows, width), jnp.float32 if keep else jnp.bfloat16
        ),
        scratch_shapes=[pltpu.VMEM((degree * CHUNK, width), jnp.float32)] * 2,
        compiler_params=pltpu.CompilerParams(vmem_limit_bytes=VMEM_LIMIT),
        cost_estimate=pl.CostEstimate(
            flops=2 * edges * width * width,
            bytes_accessed=table.shape[0] * width * 4 + count_rows * width * 6,
            transcendentals=2 * edges * width,
        ),
    )(order, states, far, own, edge_proj[2], node_proj[1], node_proj[2], bias_pair)


def pool_kernel(rows, idx_ref, own_ref, come_ref, out_ref, table, total, sems):
    @pl.when(pl.program_id(0) == 0)
    def _():
        near = own_ref.shape[0]
        first = pltpu.make_async_copy(own_ref, table.at[pl.ds(0, near)], sems.at[0])
        second = pltpu.make_async_copy(
            come_ref, table.at[pl.ds(near, come_ref.shape[0])], sems.at[1]
        )
        first.start()
        second.start()
        first.wait()
        second.wait()

    step = 32

    def some(c, carry):
        start = pl.multiple_of(c * step, step)
        for j in range(step):
            base = start * RATIO + j * RATIO
            parts = [table[idx_ref[base + k]] for k in range(RATIO)]
            while len(parts) > 1:
                parts = [a + b for a, b in zip(parts[::2], parts[1::2])]
            total[j : j + 1, :] = parts[0]
        out_ref[pl.ds(start, step), :] = (total[...] * (1.0 / RATIO)).astype(out_ref.dtype)
        return carry

    lax.fori_loop(0, rows // step, some, 0)


def pool(own, come, grouped, coarse_rows):
    width = own.shape[-1]
    rows = min(512, coarse_rows)
    return pl.pallas_call(
        functools.partial(pool_kernel, rows),
        grid=(coarse_rows // rows,),
        in_specs=[
            pl.BlockSpec((rows * RATIO,), lambda i: (i,), memory_space=pltpu.SMEM),
            pl.BlockSpec(memory_space=pl.ANY),
            pl.BlockSpec(memory_space=pl.ANY),
        ],
        out_specs=pl.BlockSpec((rows, width), lambda i: (i, 0)),
        out_shape=jax.ShapeDtypeStruct((coarse_rows, width), jnp.bfloat16),
        scratch_shapes=[
            pltpu.VMEM((own.shape[0] + come.shape[0], 1, width), jnp.float32),
            pltpu.VMEM((32, width), jnp.float32),
            pltpu.SemaphoreType.DMA((2,)),
        ],
        compiler_params=pltpu.CompilerParams(vmem_limit_bytes=VMEM_LIMIT),
    )(grouped, own, come)


def spread_kernel(rows, idx_ref, fine_ref, table_ref, out_ref, even):
    step = even.shape[0]

    def some(c, carry):
        start = pl.multiple_of(c * step, step)
        for j in range(step):
            even[j : j + 1, :] = table_ref[idx_ref[start + j]]
        out_ref[pl.ds(start, step), :] = (fine_ref[pl.ds(start, step), :] + even[...]).astype(
            out_ref.dtype
        )
        return carry

    lax.fori_loop(0, rows // step, some, 0)


def spread(fine, table, index):
    count_rows, width = fine.shape
    rows = min(2048, count_rows)
    return pl.pallas_call(
        functools.partial(spread_kernel, rows),
        grid=(count_rows // rows,),
        in_specs=[
            pl.BlockSpec((rows,), lambda i: (i,), memory_space=pltpu.SMEM),
            pl.BlockSpec((rows, width), lambda i: (i, 0)),
            pl.BlockSpec(memory_space=pltpu.VMEM),
        ],
        out_specs=pl.BlockSpec((rows, width), lambda i: (i, 0)),
        out_shape=jax.ShapeDtypeStruct((count_rows, width), jnp.bfloat16),
        scratch_shapes=[pltpu.VMEM((128, width), jnp.float32)],
        compiler_params=pltpu.CompilerParams(vmem_limit_bytes=VMEM_LIMIT),
    )(index, fine, table.reshape(table.shape[0], 1, width))


def from_behind(block, distance):
    count = lax.axis_size(AXES)
    return lax.ppermute(block, AXES, [((i - distance) % count, i) for i in range(count)])


def extended(table, block):
    return jnp.concatenate([table, from_behind(block, 1), block, from_behind(block, -1)], axis=0)


def on_device(
    features,
    fine_nbrs,
    send_rows,
    cluster,
    coarse_send,
    coarse_nbrs,
    edge_weights,
    node_weights,
    biases,
):
    local_rows, width = features.shape
    coarse_rows = local_rows // RATIO
    spill = local_rows // 32
    local_count = local_rows - (REACH - 1) * spill
    neighbor_table = extended(features, features[send_rows])

    num_parts = lax.axis_size(AXES)
    position = lax.axis_index(AXES)
    reach_index = (cluster // coarse_rows - position) % num_parts
    slot_index = cluster % coarse_rows
    combined = reach_index * coarse_rows + slot_index
    place = jnp.arange(local_rows, dtype=jnp.int32)
    ordering = lax.sort(reach_index * local_rows + place, is_stable=False)
    remote = ordering[local_count:] % local_rows
    leaving_slots = slot_index[remote]
    arrived_slots = [
        from_behind(leaving_slots[(d - 1) * spill : d * spill], d) for d in range(1, REACH)
    ]
    keys = jnp.concatenate(
        [jnp.where(reach_index == 0, slot_index, coarse_rows)] + arrived_slots, axis=0
    )
    members = 2 * local_rows
    grouped = lax.sort(
        keys * members + jnp.arange(keys.shape[0], dtype=jnp.int32), is_stable=False
    )[: coarse_rows * RATIO] % members

    fine_out = message_layer(
        features, neighbor_table, fine_nbrs, edge_weights[0], node_weights[0], biases[0], True
    )
    leaving_rows = fine_out[remote].astype(jnp.bfloat16)
    arrived_rows = jnp.concatenate(
        [from_behind(leaving_rows[(d - 1) * spill : d * spill], d) for d in range(1, REACH)], axis=0
    ).astype(jnp.float32)
    coarse_in = pool(
        fine_out.reshape(local_rows, 1, width),
        arrived_rows.reshape(-1, 1, width),
        grouped,
        coarse_rows,
    )
    coarse_table = extended(coarse_in, coarse_in[coarse_send])
    coarse_update = message_layer(
        coarse_in, coarse_table, coarse_nbrs, edge_weights[1], node_weights[1], biases[1], False
    )
    lookup = jnp.concatenate(
        [coarse_update] + [from_behind(coarse_update, -d) for d in range(1, REACH)], axis=0
    ).astype(jnp.float32)
    nodes = spread(fine_out, lookup, combined)
    return (nodes, coarse_update)


def solution(mesh):
    spread_over = ("groups", "dom", "sub")
    return jax.shard_map(
        on_device,
        mesh=mesh,
        in_specs=(
            P(spread_over, None),
            P(None, spread_over),
            P(spread_over),
            P(spread_over),
            P(spread_over),
            P(None, spread_over),
            P(),
            P(),
            P(),
        ),
        out_specs=(P(spread_over, None), P(spread_over, None)),
        check_vma=False,
    )
```

```python
import functools

import jax
import jax.numpy as jnp
from jax import lax
from jax.experimental import pallas as pl
from jax.experimental.pallas import tpu as pltpu
from jax.sharding import PartitionSpec as P

RATIO = 8
REACH = 4
AXES = ("dom", "sub")
VMEM_LIMIT = 48 * 1024 * 1024
CHUNK = 128


def half_silu(half):
    return half + half * jnp.tanh(half)


def layer_kernel(
    degree, rows, keep, idx_ref, z_ref, far_ref, own_ref, mid_ref, mix_ref, last_ref, bias_ref, out_ref, *rest
):
    rounded_ref = None if keep else rest[0]
    even, odd = rest[-2:]
    count = rows // CHUNK

    def gather(chunk, target, degrees=range(degree)):
        base = chunk * CHUNK
        for k in degrees:
            for j in range(CHUNK):
                r = k * CHUNK + j
                target[r : r + 1, :] = far_ref[idx_ref[base + (k * rows + j)]]

    def compute(chunk, source, following, target):
        start = pl.multiple_of(chunk * CHUNK, CHUNK)
        z = z_ref[pl.ds(start, CHUNK), :]
        both = jnp.dot(z, own_ref[...], preferred_element_type=jnp.float32)
        width = z.shape[1]
        own = 0.5 * (both[:, :width] + bias_ref[0:1, :])
        node = both[:, width:] + bias_ref[1:2, :]
        agg = None
        for k in range(degree):
            gather(following, target, (k,))
            hidden = half_silu(source[k * CHUNK : (k + 1) * CHUNK, :] + own).astype(jnp.bfloat16)
            msg = half_silu(
                0.5 * jnp.dot(hidden, mid_ref[...], preferred_element_type=jnp.float32)
            )
            agg = msg if agg is None else agg + msg
        pre = node + jnp.dot(
            agg.astype(jnp.bfloat16), mix_ref[...], preferred_element_type=jnp.float32
        )
        inner = half_silu(0.5 * pre).astype(jnp.bfloat16)
        update = jnp.dot(inner, last_ref[...], preferred_element_type=jnp.float32)
        if keep:
            update = (z.astype(jnp.float32) + update).astype(jnp.bfloat16)
        else:
            rounded_ref[pl.ds(start, CHUNK), :] = update.astype(jnp.bfloat16)
            update = update.astype(jnp.bfloat16)
        out_ref[pl.ds(start, CHUNK), :] = update.astype(jnp.float32)

    gather(0, even)

    def pair(p, carry):
        first = p * 2
        compute(first, even, first + 1, odd)
        compute(first + 1, odd, jnp.minimum(first + 2, count - 1), even)
        return carry

    lax.fori_loop(0, count // 2, pair, 0)


def by_row(table):
    return lax.optimization_barrier(table).reshape(table.shape[0], 1, table.shape[1])


def message_layer(states, table, neighbor_idx, edge_proj, node_proj, bias_pair, keep):
    count_rows, width = states.shape
    degree = neighbor_idx.shape[0]
    rows = min(2048, count_rows)
    blocks = count_rows // rows
    far = 0.5 * jnp.dot(table, edge_proj[1], preferred_element_type=jnp.float32)
    far = by_row(far)
    order = neighbor_idx.reshape(degree, blocks, rows).transpose(1, 0, 2).reshape(-1)
    own = jnp.concatenate([edge_proj[0], node_proj[0]], axis=1)
    whole = pl.BlockSpec(memory_space=pltpu.VMEM)
    edges = count_rows * degree
    kinds = (jnp.float32,) if keep else (jnp.float32, jnp.bfloat16)
    return pl.pallas_call(
        functools.partial(layer_kernel, degree, rows, keep),
        grid=(blocks,),
        in_specs=[
            pl.BlockSpec((degree * rows,), lambda i: (i,), memory_space=pltpu.SMEM),
            pl.BlockSpec((rows, width), lambda i: (i, 0)),
            whole,
            whole,
            whole,
            whole,
            whole,
            whole,
        ],
        out_specs=[pl.BlockSpec((rows, width), lambda i: (i, 0))] * len(kinds),
        out_shape=[jax.ShapeDtypeStruct((count_rows, width), kind) for kind in kinds],
        scratch_shapes=[pltpu.VMEM((degree * CHUNK, width), jnp.float32)] * 2,
        compiler_params=pltpu.CompilerParams(vmem_limit_bytes=VMEM_LIMIT),
        cost_estimate=pl.CostEstimate(
            flops=2 * edges * width * width,
            bytes_accessed=table.shape[0] * width * 4 + count_rows * width * 6,
            transcendentals=2 * edges * width,
        ),
    )(order, states, far, own, edge_proj[2], node_proj[1], node_proj[2], bias_pair)


def pool_kernel(rows, idx_ref, own_ref, come_ref, out_ref, table, total, sems):
    @pl.when(pl.program_id(0) == 0)
    def _():
        near = own_ref.shape[0]
        first = pltpu.make_async_copy(own_ref, table.at[pl.ds(0, near)], sems.at[0])
        second = pltpu.make_async_copy(
            come_ref, table.at[pl.ds(near, come_ref.shape[0])], sems.at[1]
        )
        first.start()
        second.start()
        first.wait()
        second.wait()

    step = 32

    def some(c, carry):
        start = pl.multiple_of(c * step, step)
        for j in range(step):
            base = start * RATIO + j * RATIO
            parts = [table[idx_ref[base + k]] for k in range(RATIO)]
            while len(parts) > 1:
                parts = [a + b for a, b in zip(parts[::2], parts[1::2])]
            total[j : j + 1, :] = parts[0]
        out_ref[pl.ds(start, step), :] = (total[...] * (1.0 / RATIO)).astype(out_ref.dtype)
        return carry

    lax.fori_loop(0, rows // step, some, 0)


def pool(own, come, grouped, coarse_rows):
    width = own.shape[-1]
    rows = min(512, coarse_rows)
    return pl.pallas_call(
        functools.partial(pool_kernel, rows),
        grid=(coarse_rows // rows,),
        in_specs=[
            pl.BlockSpec((rows * RATIO,), lambda i: (i,), memory_space=pltpu.SMEM),
            pl.BlockSpec(memory_space=pl.ANY),
            pl.BlockSpec(memory_space=pl.ANY),
        ],
        out_specs=pl.BlockSpec((rows, width), lambda i: (i, 0)),
        out_shape=jax.ShapeDtypeStruct((coarse_rows, width), jnp.bfloat16),
        scratch_shapes=[
            pltpu.VMEM((own.shape[0] + come.shape[0], 1, width), jnp.float32),
            pltpu.VMEM((32, width), jnp.float32),
            pltpu.SemaphoreType.DMA((2,)),
        ],
        compiler_params=pltpu.CompilerParams(vmem_limit_bytes=VMEM_LIMIT),
    )(grouped, own, come)


def spread_kernel(rows, near, far, idx_ref, fine_ref, own_ref, come_ref, out_ref, table, even, sems):
    @pl.when(pl.program_id(0) == 0)
    def _():
        first = pltpu.make_async_copy(own_ref, table.at[pl.ds(0, near)], sems.at[0])
        second = pltpu.make_async_copy(come_ref, table.at[pl.ds(near, far)], sems.at[1])
        first.start()
        second.start()
        first.wait()
        second.wait()

    step = even.shape[0]

    def some(c, carry):
        start = pl.multiple_of(c * step, step)
        for j in range(step):
            even[j : j + 1, :] = table[idx_ref[start + j]]
        out_ref[pl.ds(start, step), :] = (fine_ref[pl.ds(start, step), :] + even[...]).astype(
            out_ref.dtype
        )
        return carry

    lax.fori_loop(0, rows // step, some, 0)


def spread(fine, own, come, index):
    count_rows, width = fine.shape
    rows = min(2048, count_rows)
    near, far = own.shape[0], come.shape[0]
    return pl.pallas_call(
        functools.partial(spread_kernel, rows, near, far),
        grid=(count_rows // rows,),
        in_specs=[
            pl.BlockSpec((rows,), lambda i: (i,), memory_space=pltpu.SMEM),
            pl.BlockSpec((rows, width), lambda i: (i, 0)),
            pl.BlockSpec(memory_space=pl.ANY),
            pl.BlockSpec(memory_space=pl.ANY),
        ],
        out_specs=pl.BlockSpec((rows, width), lambda i: (i, 0)),
        out_shape=jax.ShapeDtypeStruct((count_rows, width), jnp.bfloat16),
        scratch_shapes=[
            pltpu.VMEM((near + far, 1, width), jnp.float32),
            pltpu.VMEM((128, width), jnp.float32),
            pltpu.SemaphoreType.DMA((2,)),
        ],
        compiler_params=pltpu.CompilerParams(vmem_limit_bytes=VMEM_LIMIT),
    )(index, fine, own, come)


def ranks(reach_index):
    lanes = 128
    hit = (reach_index[None] == jnp.arange(1, REACH, dtype=jnp.int32)[:, None]).astype(jnp.bfloat16)
    hit = hit.reshape(REACH - 1, -1, lanes)
    lines = hit.shape[1]
    before = jnp.triu(jnp.ones((lanes, lanes), jnp.bfloat16), 1)
    above = jnp.tril(jnp.ones((lines, lines), jnp.bfloat16), -1)
    inside = jnp.einsum("dri,ij->drj", hit, before, preferred_element_type=jnp.float32)
    sums = jnp.sum(hit.astype(jnp.float32), axis=2).astype(jnp.bfloat16)
    ahead = jnp.einsum("rs,ds->dr", above, sums, preferred_element_type=jnp.float32)
    rank = (inside + ahead[:, :, None]) * hit.astype(jnp.float32)
    return jnp.sum(rank, axis=0).reshape(-1).astype(jnp.int32)


def from_behind(block, distance):
    count = lax.axis_size(AXES)
    return lax.ppermute(block, AXES, [((i - distance) % count, i) for i in range(count)])


def extended(table, block):
    return jnp.concatenate([table, from_behind(block, 1), block, from_behind(block, -1)], axis=0)


def on_device(
    features,
    fine_nbrs,
    send_rows,
    cluster,
    coarse_send,
    coarse_nbrs,
    edge_weights,
    node_weights,
    biases,
):
    local_rows, width = features.shape
    coarse_rows = local_rows // RATIO
    spill = local_rows // 32
    local_count = local_rows - (REACH - 1) * spill
    neighbor_table = extended(features, features[send_rows])

    num_parts = lax.axis_size(AXES)
    position = lax.axis_index(AXES)
    reach_index = (cluster // coarse_rows - position) % num_parts
    slot_index = cluster % coarse_rows
    wanted = jnp.where(
        reach_index == 0,
        slot_index,
        coarse_rows + (reach_index - 1) * spill + ranks(reach_index),
    )
    place = jnp.arange(local_rows, dtype=jnp.int32)
    ordering = lax.sort(
        (reach_index * local_rows + place) * coarse_rows + slot_index, is_stable=False
    )
    leaving = ordering[local_count:]
    remote = leaving // coarse_rows % local_rows
    leaving_slots = leaving % coarse_rows
    arrived_slots = [
        from_behind(leaving_slots[(d - 1) * spill : d * spill], d) for d in range(1, REACH)
    ]
    keys = jnp.concatenate(
        [jnp.where(reach_index == 0, slot_index, coarse_rows)] + arrived_slots, axis=0
    )
    members = 2 * local_rows
    grouped = lax.sort(
        keys * members + jnp.arange(keys.shape[0], dtype=jnp.int32), is_stable=False
    )[: coarse_rows * RATIO] % members

    (fine_out,) = message_layer(
        features, neighbor_table, fine_nbrs, edge_weights[0], node_weights[0], biases[0], True
    )
    leaving_rows = fine_out[remote].astype(jnp.bfloat16)
    arrived_rows = jnp.concatenate(
        [from_behind(leaving_rows[(d - 1) * spill : d * spill], d) for d in range(1, REACH)], axis=0
    ).astype(jnp.float32)
    coarse_in = pool(by_row(fine_out), by_row(arrived_rows), grouped, coarse_rows)
    coarse_table = extended(coarse_in, coarse_in[coarse_send])
    coarse_float, coarse_update = message_layer(
        coarse_in, coarse_table, coarse_nbrs, edge_weights[1], node_weights[1], biases[1], False
    )
    answers = coarse_update[jnp.concatenate(arrived_slots)]
    returned = jnp.concatenate(
        [from_behind(answers[(d - 1) * spill : d * spill], -d) for d in range(1, REACH)], axis=0
    ).astype(jnp.float32)
    nodes = spread(fine_out, by_row(coarse_float), by_row(returned), wanted)
    return (nodes, coarse_update)


def solution(mesh):
    spread_over = ("groups", "dom", "sub")
    return jax.shard_map(
        on_device,
        mesh=mesh,
        in_specs=(
            P(spread_over, None),
            P(None, spread_over),
            P(spread_over),
            P(spread_over),
            P(spread_over),
            P(None, spread_over),
            P(),
            P(),
            P(),
        ),
        out_specs=(P(spread_over, None), P(spread_over, None)),
        check_vma=False,
    )
```

```python
import functools

import jax
import jax.numpy as jnp
from jax import lax
from jax.experimental import pallas as pl
from jax.experimental.pallas import tpu as pltpu
from jax.sharding import PartitionSpec as P

RATIO = 8
REACH = 4
AXES = ("dom", "sub")
VMEM_LIMIT = 48 * 1024 * 1024
CHUNK = 128


def half_silu(half):
    return half + half * jnp.tanh(half)


def layer_kernel(
    degree, rows, keep, idx_ref, z_ref, far_ref, own_ref, mid_ref, mix_ref, last_ref, bias_ref, out_ref, *rest
):
    rounded_ref = None if keep else rest[0]
    even, odd = rest[-2:]
    count = rows // CHUNK

    edges = degree * CHUNK
    share = -(-edges // (degree + 3))

    def gather(chunk, target, low, high):
        base = chunk * CHUNK
        for r in range(low, min(high, edges)):
            k, j = divmod(r, CHUNK)
            target[r : r + 1, :] = far_ref[idx_ref[base + (k * rows + j)]]

    def compute(chunk, source, following, target):
        start = pl.multiple_of(chunk * CHUNK, CHUNK)
        z = z_ref[pl.ds(start, CHUNK), :]
        both = jnp.dot(z, own_ref[...], preferred_element_type=jnp.float32)
        gather(following, target, 0, share)
        width = z.shape[1]
        own = 0.5 * (both[:, :width] + bias_ref[0:1, :])
        node = both[:, width:] + bias_ref[1:2, :]
        agg = None
        for k in range(degree):
            hidden = half_silu(source[k * CHUNK : (k + 1) * CHUNK, :] + own).astype(jnp.bfloat16)
            product = jnp.dot(hidden, mid_ref[...], preferred_element_type=jnp.float32)
            gather(following, target, (k + 1) * share, (k + 2) * share)
            msg = half_silu(0.5 * product)
            agg = msg if agg is None else agg + msg
        pre = node + jnp.dot(
            agg.astype(jnp.bfloat16), mix_ref[...], preferred_element_type=jnp.float32
        )
        gather(following, target, (degree + 1) * share, (degree + 2) * share)
        inner = half_silu(0.5 * pre).astype(jnp.bfloat16)
        update = jnp.dot(inner, last_ref[...], preferred_element_type=jnp.float32)
        gather(following, target, (degree + 2) * share, edges)
        if keep:
            update = (z.astype(jnp.float32) + update).astype(jnp.bfloat16)
        else:
            rounded_ref[pl.ds(start, CHUNK), :] = update.astype(jnp.bfloat16)
            update = update.astype(jnp.bfloat16)
        out_ref[pl.ds(start, CHUNK), :] = update.astype(jnp.float32)

    gather(0, even, 0, edges)

    def pair(p, carry):
        first = p * 2
        compute(first, even, first + 1, odd)
        compute(first + 1, odd, jnp.minimum(first + 2, count - 1), even)
        return carry

    lax.fori_loop(0, count // 2, pair, 0)


def far_kernel(states_ref, low_ref, mine_ref, high_ref, proj_ref, out_ref):
    count, tile = states_ref.shape[0], 1024

    def some(c, carry):
        start = pl.multiple_of(c * tile, tile)
        out_ref[pl.ds(start, tile), :] = 0.5 * jnp.dot(
            states_ref[pl.ds(start, tile), :], proj_ref[...], preferred_element_type=jnp.float32
        )
        return carry

    lax.fori_loop(0, count // tile, some, 0)
    size = low_ref.shape[0]
    for n, part in enumerate((low_ref, mine_ref, high_ref)):
        out_ref[count + n * size : count + (n + 1) * size, :] = 0.5 * jnp.dot(
            part[...], proj_ref[...], preferred_element_type=jnp.float32
        )


def far_table(states, halo, proj):
    whole = pl.BlockSpec(memory_space=pltpu.VMEM)
    rows = states.shape[0] + sum(part.shape[0] for part in halo)
    return pl.pallas_call(
        far_kernel,
        in_specs=[whole] * 5,
        out_specs=whole,
        out_shape=jax.ShapeDtypeStruct((rows, states.shape[1]), jnp.float32),
        compiler_params=pltpu.CompilerParams(vmem_limit_bytes=VMEM_LIMIT),
    )(states, *halo, proj)


def by_row(table):
    return lax.optimization_barrier(table).reshape(table.shape[0], 1, table.shape[1])


def message_layer(states, halo, neighbor_idx, edge_proj, node_proj, bias_pair, keep):
    count_rows, width = states.shape
    degree = neighbor_idx.shape[0]
    rows = min(2048, count_rows)
    blocks = count_rows // rows
    table = far_table(states, halo, edge_proj[1])
    far = by_row(table)
    order = neighbor_idx.reshape(degree, blocks, rows).transpose(1, 0, 2).reshape(-1)
    own = jnp.concatenate([edge_proj[0], node_proj[0]], axis=1)
    whole = pl.BlockSpec(memory_space=pltpu.VMEM)
    edges = count_rows * degree
    kinds = (jnp.float32,) if keep else (jnp.float32, jnp.bfloat16)
    return pl.pallas_call(
        functools.partial(layer_kernel, degree, rows, keep),
        grid=(blocks,),
        in_specs=[
            pl.BlockSpec((degree * rows,), lambda i: (i,), memory_space=pltpu.SMEM),
            pl.BlockSpec((rows, width), lambda i: (i, 0)),
            whole,
            whole,
            whole,
            whole,
            whole,
            whole,
        ],
        out_specs=[pl.BlockSpec((rows, width), lambda i: (i, 0))] * len(kinds),
        out_shape=[jax.ShapeDtypeStruct((count_rows, width), kind) for kind in kinds],
        scratch_shapes=[pltpu.VMEM((degree * CHUNK, width), jnp.float32)] * 2,
        compiler_params=pltpu.CompilerParams(vmem_limit_bytes=VMEM_LIMIT),
        cost_estimate=pl.CostEstimate(
            flops=2 * edges * width * width,
            bytes_accessed=table.shape[0] * width * 4 + count_rows * width * 6,
            transcendentals=2 * edges * width,
        ),
    )(order, states, far, own, edge_proj[2], node_proj[1], node_proj[2], bias_pair)


def pool_kernel(rows, idx_ref, own_ref, come_ref, out_ref, table, total, sems):
    @pl.when(pl.program_id(0) == 0)
    def _():
        near = own_ref.shape[0]
        first = pltpu.make_async_copy(own_ref, table.at[pl.ds(0, near)], sems.at[0])
        second = pltpu.make_async_copy(
            come_ref, table.at[pl.ds(near, come_ref.shape[0])], sems.at[1]
        )
        first.start()
        second.start()
        first.wait()
        second.wait()

    step = 32

    def some(c, carry):
        start = pl.multiple_of(c * step, step)
        for j in range(step):
            base = start * RATIO + j * RATIO
            parts = [table[idx_ref[base + k]] for k in range(RATIO)]
            while len(parts) > 1:
                parts = [a + b for a, b in zip(parts[::2], parts[1::2])]
            total[j : j + 1, :] = parts[0]
        out_ref[pl.ds(start, step), :] = (total[...] * (1.0 / RATIO)).astype(out_ref.dtype)
        return carry

    lax.fori_loop(0, rows // step, some, 0)


def pool(own, come, grouped, coarse_rows):
    width = own.shape[-1]
    rows = min(512, coarse_rows)
    return pl.pallas_call(
        functools.partial(pool_kernel, rows),
        grid=(coarse_rows // rows,),
        in_specs=[
            pl.BlockSpec((rows * RATIO,), lambda i: (i,), memory_space=pltpu.SMEM),
            pl.BlockSpec(memory_space=pl.ANY),
            pl.BlockSpec(memory_space=pl.ANY),
        ],
        out_specs=pl.BlockSpec((rows, width), lambda i: (i, 0)),
        out_shape=jax.ShapeDtypeStruct((coarse_rows, width), jnp.bfloat16),
        scratch_shapes=[
            pltpu.VMEM((own.shape[0] + come.shape[0], 1, width), jnp.float32),
            pltpu.VMEM((32, width), jnp.float32),
            pltpu.SemaphoreType.DMA((2,)),
        ],
        compiler_params=pltpu.CompilerParams(vmem_limit_bytes=VMEM_LIMIT),
    )(grouped, own, come)


def spread_kernel(rows, near, far, idx_ref, fine_ref, own_ref, come_ref, out_ref, table, even, sems):
    @pl.when(pl.program_id(0) == 0)
    def _():
        first = pltpu.make_async_copy(own_ref, table.at[pl.ds(0, near)], sems.at[0])
        second = pltpu.make_async_copy(come_ref, table.at[pl.ds(near, far)], sems.at[1])
        first.start()
        second.start()
        first.wait()
        second.wait()

    step = even.shape[0]

    def some(c, carry):
        start = pl.multiple_of(c * step, step)
        for j in range(step):
            even[j : j + 1, :] = table[idx_ref[start + j]]
        out_ref[pl.ds(start, step), :] = (fine_ref[pl.ds(start, step), :] + even[...]).astype(
            out_ref.dtype
        )
        return carry

    lax.fori_loop(0, rows // step, some, 0)


def spread(fine, own, come, index):
    count_rows, width = fine.shape
    rows = min(2048, count_rows)
    near, far = own.shape[0], come.shape[0]
    return pl.pallas_call(
        functools.partial(spread_kernel, rows, near, far),
        grid=(count_rows // rows,),
        in_specs=[
            pl.BlockSpec((rows,), lambda i: (i,), memory_space=pltpu.SMEM),
            pl.BlockSpec((rows, width), lambda i: (i, 0)),
            pl.BlockSpec(memory_space=pl.ANY),
            pl.BlockSpec(memory_space=pl.ANY),
        ],
        out_specs=pl.BlockSpec((rows, width), lambda i: (i, 0)),
        out_shape=jax.ShapeDtypeStruct((count_rows, width), jnp.bfloat16),
        scratch_shapes=[
            pltpu.VMEM((near + far, 1, width), jnp.float32),
            pltpu.VMEM((128, width), jnp.float32),
            pltpu.SemaphoreType.DMA((2,)),
        ],
        compiler_params=pltpu.CompilerParams(vmem_limit_bytes=VMEM_LIMIT),
    )(index, fine, own, come)


def ranks(reach_index):
    lanes = 128
    hit = (reach_index[None] == jnp.arange(1, REACH, dtype=jnp.int32)[:, None]).astype(jnp.bfloat16)
    hit = hit.reshape(REACH - 1, -1, lanes)
    lines = hit.shape[1]
    before = jnp.triu(jnp.ones((lanes, lanes), jnp.bfloat16), 1)
    above = jnp.tril(jnp.ones((lines, lines), jnp.bfloat16), -1)
    inside = jnp.einsum("dri,ij->drj", hit, before, preferred_element_type=jnp.float32)
    sums = jnp.sum(hit.astype(jnp.float32), axis=2).astype(jnp.bfloat16)
    ahead = jnp.einsum("rs,ds->dr", above, sums, preferred_element_type=jnp.float32)
    rank = (inside + ahead[:, :, None]) * hit.astype(jnp.float32)
    return jnp.sum(rank, axis=0).reshape(-1).astype(jnp.int32)


def from_behind(block, distance):
    count = lax.axis_size(AXES)
    return lax.ppermute(block, AXES, [((i - distance) % count, i) for i in range(count)])


def halo_of(block):
    return from_behind(block, 1), block, from_behind(block, -1)


def on_device(
    features,
    fine_nbrs,
    send_rows,
    cluster,
    coarse_send,
    coarse_nbrs,
    edge_weights,
    node_weights,
    biases,
):
    local_rows, width = features.shape
    coarse_rows = local_rows // RATIO
    spill = local_rows // 32
    local_count = local_rows - (REACH - 1) * spill
    fine_halo = halo_of(features[send_rows])

    num_parts = lax.axis_size(AXES)
    position = lax.axis_index(AXES)
    reach_index = (cluster // coarse_rows - position) % num_parts
    slot_index = cluster % coarse_rows
    wanted = jnp.where(
        reach_index == 0,
        slot_index,
        coarse_rows + (reach_index - 1) * spill + ranks(reach_index),
    )
    place = jnp.arange(local_rows, dtype=jnp.int32)
    ordering = lax.sort(
        (reach_index * local_rows + place) * coarse_rows + slot_index, is_stable=False
    )
    leaving = ordering[local_count:]
    remote = leaving // coarse_rows % local_rows
    leaving_slots = leaving % coarse_rows
    arrived_slots = [
        from_behind(leaving_slots[(d - 1) * spill : d * spill], d) for d in range(1, REACH)
    ]
    keys = jnp.concatenate(
        [jnp.where(reach_index == 0, slot_index, coarse_rows)] + arrived_slots, axis=0
    )
    members = 2 * local_rows
    grouped = lax.sort(
        keys * members + jnp.arange(keys.shape[0], dtype=jnp.int32), is_stable=False
    )[: coarse_rows * RATIO] % members

    (fine_out,) = message_layer(
        features, fine_halo, fine_nbrs, edge_weights[0], node_weights[0], biases[0], True
    )
    leaving_rows = fine_out[remote].astype(jnp.bfloat16)
    arrived_rows = jnp.concatenate(
        [from_behind(leaving_rows[(d - 1) * spill : d * spill], d) for d in range(1, REACH)], axis=0
    ).astype(jnp.float32)
    coarse_in = pool(by_row(fine_out), by_row(arrived_rows), grouped, coarse_rows)
    coarse_halo = halo_of(coarse_in[coarse_send])
    coarse_float, coarse_update = message_layer(
        coarse_in, coarse_halo, coarse_nbrs, edge_weights[1], node_weights[1], biases[1], False
    )
    answers = coarse_update[jnp.concatenate(arrived_slots)]
    returned = jnp.concatenate(
        [from_behind(answers[(d - 1) * spill : d * spill], -d) for d in range(1, REACH)], axis=0
    ).astype(jnp.float32)
    nodes = spread(fine_out, by_row(coarse_float), by_row(returned), wanted)
    return (nodes, coarse_update)


def solution(mesh):
    spread_over = ("groups", "dom", "sub")
    return jax.shard_map(
        on_device,
        mesh=mesh,
        in_specs=(
            P(spread_over, None),
            P(None, spread_over),
            P(spread_over),
            P(spread_over),
            P(spread_over),
            P(None, spread_over),
            P(),
            P(),
            P(),
        ),
        out_specs=(P(spread_over, None), P(spread_over, None)),
        check_vma=False,
    )
```
